32 devices in a mesh: leaf: 8 (over y, x, core), rhs: 4 (over z).
Axes of the slice: x: 2, y: 2, z: 4, core: 2. Of those that a mesh axis runs over, the one named last changes fastest.
Arguments:
- rhs_cols: bfloat16 [65536, 512], P('leaf', 'rhs'), may hold values from -6 to 6
- leaf_inv: bfloat16 [128, 512, 512], P('leaf', 'rhs')
- leaf_basis: bfloat16 [128, 512, 128], P('leaf'), may hold values from -0.25 to 0.25
- leaf_back: bfloat16 [128, 512, 128], P('leaf'), may hold values from -0.5 to 0.5
- leaf_coarse: float32 [128, 128, 128], P('leaf')
- mid_inv: float32 [120, 256, 256], P('leaf')
- mid_basis: float32 [120, 256, 128], P('leaf'), may hold values from -0.375 to 0.375
- mid_back: float32 [120, 256, 128], P('leaf'), may hold values from -0.5 to 0.5
- mid_coarse: float32 [120, 128, 128], P('leaf')
- top_inv: float32 [8, 256, 256], P('leaf')
- top_basis: float32 [8, 256, 128], P('leaf'), may hold values from -0.375 to 0.375
- top_back: float32 [8, 256, 128], P('leaf'), may hold values from -0.5 to 0.5
- top_coarse: float32 [8, 128, 128], P('leaf')
Outputs:
- solution: float32 [65536, 512], P('leaf', 'rhs')
The draws below stay inside these ranges and needn't reach their ends.
All inputs are finite; a program needn't handle non-finite values.
Results may differ from the reference program's by a relative error of at most 0.004.
Values may be sent and summed in bfloat16 or wider, within the bound.
A program may use at most 192 MiB of HBM per device.

```python
import jax
import jax.numpy as jnp
import numpy as np
from jax import lax

LEAF = 512
RANK = 128
RHS = 512
LEAF_DEV = 16
LEAVES = 128
POINTS = 65536
MIDS = 120
N_LEAF = 8


def dominant(key, count, order, salt):
    first_key, second_key = jax.random.split(jax.random.fold_in(key, salt))
    spread = jax.random.normal(first_key, (count, order, order), jnp.float32) * (0.3 / order ** 0.5)
    diagonal = jax.random.uniform(second_key, (count, order), jnp.float32, 0.7, 1.2)
    identity = jnp.eye(order, dtype=jnp.float32)
    return spread * (1.0 - identity) + identity * diagonal[:, None, :]


def draw_leaf_inv(key, part):
    return dominant(key, LEAVES, LEAF, 101).astype(jnp.bfloat16)


def draw_leaf_coarse(key, part):
    return dominant(key, LEAVES, RANK, 202)


def draw_mid_inv(key, part):
    return dominant(key, MIDS, 2 * RANK, 303)


def draw_mid_coarse(key, part):
    return dominant(key, MIDS, RANK, 404)


def draw_top_inv(key, part):
    return dominant(key, N_LEAF, 2 * RANK, 505)


def draw_top_coarse(key, part):
    return dominant(key, N_LEAF, RANK, 606)


def block_scale(own_key, dims, cuts, smallest, high):
    def one(dim, parts):
        steps = jax.random.uniform(jax.random.fold_in(jax.random.fold_in(own_key, 6), dim), (parts,), jnp.float32, smallest / len(cuts), high / len(cuts))
        return jnp.repeat(jnp.exp(steps), dims[dim] // parts).reshape((-1,) + (1,) * (len(dims) - dim - 1))

    level = one(*cuts[0])
    for cut in cuts[1:]:
        level = level * one(*cut)
    return level


def scatter_about(key, extent, deviation, most, pieces=(), kind=jnp.bfloat16):
    loudness = block_scale(key, extent, pieces, -0.22, 0.18) if pieces else 1.0
    values = jax.random.normal(key, extent, jnp.float32) * deviation * loudness
    return jnp.minimum(jnp.maximum(values, -most), most).astype(kind)


def setup_inputs(seed: int = 0) -> dict:
    key_of = jax.random.split(jax.random.key(seed), 14)
    rhs_cols = scatter_about(key_of[0], (POINTS, RHS), 1.0, 6.0, ((0, 8), (1, 4)))
    leaf_inv = draw_leaf_inv(jax.random.fold_in(key_of[13], 71), 0)
    leaf_basis = scatter_about(key_of[2], (LEAVES, LEAF, RANK), LEAF ** -0.5, 0.25, ((0, 8),))
    leaf_back = scatter_about(key_of[3], (LEAVES, LEAF, RANK), RANK ** -0.5, 0.5, ((0, 8),))
    leaf_coarse = draw_leaf_coarse(jax.random.fold_in(key_of[13], 71), 0)
    mid_inv = draw_mid_inv(jax.random.fold_in(key_of[13], 71), 0)
    mid_basis = scatter_about(key_of[6], (MIDS, 2 * RANK, RANK), (2 * RANK) ** -0.5, 0.375, ((0, 8),), jnp.float32)
    mid_back = scatter_about(key_of[7], (MIDS, 2 * RANK, RANK), RANK ** -0.5, 0.5, ((0, 8),), jnp.float32)
    mid_coarse = draw_mid_coarse(jax.random.fold_in(key_of[13], 71), 0)
    top_inv = draw_top_inv(jax.random.fold_in(key_of[13], 71), 0)
    top_basis = scatter_about(key_of[10], (N_LEAF, 2 * RANK, RANK), (2 * RANK) ** -0.5, 0.375, ((0, 8),), jnp.float32)
    top_back = scatter_about(key_of[11], (N_LEAF, 2 * RANK, RANK), RANK ** -0.5, 0.5, ((0, 8),), jnp.float32)
    top_coarse = draw_top_coarse(jax.random.fold_in(key_of[13], 71), 0)
    return dict(rhs_cols=rhs_cols, leaf_inv=leaf_inv, leaf_basis=leaf_basis, leaf_back=leaf_back, leaf_coarse=leaf_coarse, mid_inv=mid_inv, mid_basis=mid_basis, mid_back=mid_back, mid_coarse=mid_coarse, top_inv=top_inv, top_basis=top_basis, top_back=top_back, top_coarse=top_coarse)


exact_mode = lax.Precision.HIGHEST


def node_up(inverse, basis_mat, coarse, stacked):
    solved = jnp.einsum('nij,njc->nic', inverse, stacked, precision=exact_mode)
    reduced = jnp.einsum('nik,nic->nkc', basis_mat, solved, precision=exact_mode)
    upward = jnp.einsum('nkl,nlc->nkc', coarse, reduced, precision=exact_mode)
    return solved, reduced, upward


def node_down(solved, reduced, back_mat, parent_part):
    return solved - jnp.einsum('nik,nkc->nic', back_mat, reduced - parent_part, precision=exact_mode)


def leaf_solve(operands):
    inverse, block = operands
    return jnp.dot(inverse, block, preferred_element_type=jnp.float32).astype(jnp.bfloat16)


def reference(rhs_cols, leaf_inv, leaf_basis, leaf_back, leaf_coarse, mid_inv, mid_basis, mid_back, mid_coarse, top_inv, top_basis, top_back, top_coarse):
    blocks = rhs_cols.reshape(LEAVES, LEAF, RHS)
    leaf_vals = lax.map(leaf_solve, (leaf_inv, blocks))
    leaf_proj = jnp.einsum('nik,nic->nkc', leaf_basis.astype(jnp.float32), leaf_vals.astype(jnp.float32))
    current = jnp.einsum('nkl,nlc->nkc', leaf_coarse, leaf_proj, precision=exact_mode)
    local_levels = LEAF_DEV.bit_length() - 1
    top_levels = N_LEAF.bit_length() - 1
    total_levels = local_levels + top_levels
    stored = []
    for height in range(1, total_levels + 1):
        node_count = LEAVES >> height
        if height <= local_levels:
            per_device = LEAF_DEV >> height
            offset = LEAF_DEV - (LEAF_DEV >> (height - 1))
            index = np.array([(p // per_device) * (LEAF_DEV - 1) + offset + p % per_device for p in range(node_count)], dtype=np.int32)
            factors = (mid_inv[index], mid_basis[index], mid_back[index], mid_coarse[index])
        else:
            upper = height - local_levels
            index = np.arange(node_count, dtype=np.int32) * (1 << upper) + (1 << (upper - 1))
            factors = (top_inv[index], top_basis[index], top_back[index], top_coarse[index])
        stacked = current.reshape(node_count, 2 * RANK, RHS)
        solved, reduced, current = node_up(factors[0], factors[1], factors[2 + 1], stacked)
        stored.append((solved, reduced, factors[2]))
    parent_part = None
    for height in range(total_levels, 0, -1):
        solved, reduced, back_mat = stored[height - 1]
        if height == total_levels:
            halves = solved
        else:
            halves = node_down(solved, reduced, back_mat, parent_part)
        parent_part = halves.reshape(2 * halves.shape[0], RANK, RHS)
    difference = (leaf_proj - parent_part).astype(jnp.bfloat16)
    result = leaf_vals.astype(jnp.float32) - jnp.einsum('nik,nkc->nic', leaf_back.astype(jnp.float32), difference.astype(jnp.float32))
    return result.reshape(POINTS, RHS)
```

```python
import functools

import jax
import jax.numpy as jnp
from jax import lax
from jax.experimental import pallas as pl
from jax.experimental.pallas import tpu as pltpu
from jax.sharding import PartitionSpec as P

MESH = pl.DeviceIdType.MESH
f32, bf16 = jnp.float32, jnp.bfloat16
OWN_AHEAD, END_AHEAD, INNER_LAG, END_LAG = 4, 2, 2, 5


def split(a):
    high = a.astype(bf16)
    return high, (a - high.astype(f32)).astype(bf16)


def dot3(a, b, dims=(((1,), (0,)), ((), ()))):
    (ah, al), (bh, bl) = split(a), split(b)
    dot = functools.partial(lax.dot_general, dimension_numbers=dims, preferred_element_type=f32)
    return dot(ah, bh) + (dot(al, bh) + dot(ah, bl))


TRANSPOSED = (((0,), (0,)), ((), ()))


def tree_kernel(leaf_total, rhs, inv, basis, coarse, mid_inv, mid_basis, mid_back, mid_coarse,
                top_inv, top_basis, top_back, top_coarse, vals_out, diff_out,
                inv_v, rhs_v, rhs_far, vals, vals_far, basis_v, coarse_v, mi, mb, mk, mc, ti, tb, tk, tc,
                mid_g, mid_f, gs, acc, proj, zs, top_m, top_w, top_a, top_g, top_in,
                load, inv_s, inv_end_r, inv_mid_r, fwd_s, fwd_r, rhs_s, rhs_r, res_s, res_r,
                out_s, top_s, top_r, ex_s, ex_r):
    leaves, rows, width = inv.shape
    rank, cols = basis.shape[2], rhs.shape[2]
    levels = leaves.bit_length() - 1
    depth = leaf_total.bit_length() - 1
    pos, z = lax.axis_index("leaf"), lax.axis_index("rhs")
    inner = (z == 1) | (z == 2)
    end = jnp.logical_not(inner)
    low = z < 2
    end_z = jnp.where(low, 0, 3)
    mid_z = jnp.where(low, 1, 2)
    pair_z = jnp.where(low, 2, 1)
    pair_end = jnp.where(low, 3, 0)

    def slot(l, who):
        return inv_v.at[l, pl.ds(pl.multiple_of(who * rows, rows), rows), :]

    def remote(src, dst, s, r, where):
        return pltpu.make_async_remote_copy(src_ref=src, dst_ref=dst, send_sem=s, recv_sem=r,
                                            device_id=where, device_id_type=MESH)

    def inv_to_mid(l):
        return remote(inv.at[l], slot(l, end_z), inv_s.at[l], inv_end_r.at[l], {"rhs": mid_z})

    def inv_to_pair(l):
        return remote(inv.at[l], slot(l, z), inv_s.at[l], inv_mid_r.at[l], {"rhs": pair_z})

    def forward(l):
        return remote(slot(l, end_z), slot(l, end_z), fwd_s.at[l], fwd_r.at[l], {"rhs": pair_z})

    def rhs_to_mid(l):
        return remote(rhs.at[l], rhs_far.at[l], rhs_s.at[l], rhs_r.at[l], {"rhs": mid_z})

    def result(l):
        return remote(vals_far.at[l], vals.at[l], res_s.at[l], res_r.at[l], {"rhs": end_z})

    def vals_copy(l):
        return pltpu.make_async_copy(vals.at[l], vals_out.at[l], out_s.at[l])

    pairs = [(basis, basis_v), (coarse, coarse_v), (mid_inv, mi), (mid_basis, mb), (mid_back, mk),
             (mid_coarse, mc), (top_inv, ti), (top_basis, tb), (top_back, tk), (top_coarse, tc)]
    loads = [pltpu.make_async_copy(a, b, load.at[i]) for i, (a, b) in enumerate(pairs)]
    own_inv = pltpu.make_async_copy(
        inv, inv_v.at[:, pl.ds(pl.multiple_of(z * rows, rows), rows), :], load.at[len(pairs)])
    own_rhs = pltpu.make_async_copy(rhs, rhs_v, load.at[len(pairs) + 1])

    barrier = pltpu.get_barrier_semaphore()

    def greet(k, carry):
        pl.semaphore_signal(barrier, inc=1, device_id={"leaf": lax.rem(pos + k, leaf_total)}, device_id_type=MESH)
        return carry

    lax.fori_loop(1, leaf_total, greet, 0)

    @pl.when(inner)
    def _():
        pl.semaphore_signal(barrier, inc=1, device_id={"rhs": end_z}, device_id_type=MESH)
        pl.semaphore_signal(barrier, inc=1, device_id={"rhs": pair_z}, device_id_type=MESH)
        pl.semaphore_wait(barrier, leaf_total + 1)

    @pl.when(end)
    def _():
        pl.semaphore_signal(barrier, inc=1, device_id={"rhs": mid_z}, device_id_type=MESH)
        pl.semaphore_wait(barrier, leaf_total)

    @pl.when(inner)
    def _():
        def go(l, carry):
            inv_to_pair(l).start()
            return carry

        lax.fori_loop(0, min(OWN_AHEAD, leaves), go, 0)
        own_inv.start()
        own_rhs.start()

    @pl.when(end)
    def _():
        def go(l, carry):
            inv_to_mid(l).start()
            rhs_to_mid(l).start()
            return carry

        lax.fori_loop(0, min(END_AHEAD, leaves), go, 0)

    for copy in loads:
        copy.start()
    for copy in loads:
        copy.wait()

    @pl.when(inner)
    def _():
        own_inv.wait()
        own_rhs.wait()

    def merge(e, u, w, s):
        reduced = dot3(u, e, TRANSPOSED)
        return dot3(s, reduced), e - dot3(w, reduced)

    def top_copies(height, k):
        base = (pos // (1 << height)) * (1 << height)
        target = base + lax.rem(pos - base + k, 1 << height)
        i = height - 1
        return (remote(top_m.at[i], top_m.at[i], top_s.at[0, k], top_r.at[0, i], {"leaf": target}),
                remote(top_w.at[i], top_w.at[i], top_s.at[1, k], top_r.at[1, i], {"leaf": target}))

    for height in range(1, depth + 1):
        @pl.when(lax.rem(pos, 1 << height) == 1 << (height - 1))
        def _():
            top_w[height - 1] = tk[0]
            g_mat, f_mat = merge(ti[0], tb[0], tk[0], tc[0])
            top_m[height - 1, 0:rank, :] = g_mat
            top_m[height - 1, rank:, :] = ti[0] if height == depth else f_mat

            def go(k, carry):
                for copy in top_copies(height, k):
                    copy.start()
                return carry

            lax.fori_loop(1, 1 << height, go, 0)

    def first(height):
        return 2 * leaves - (2 * leaves >> height)

    def pair_of(height, p):
        i = first(height - 1) + 2 * p
        return jnp.concatenate([gs[i], gs[i + 1]], axis=0)

    def visits(l, body):
        for height in range(1, levels + 1):
            @pl.when(lax.rem(l + 1, 1 << height) == 0)
            def _():
                p = (l + 1) // (1 << height) - 1
                body(height, p, first(height) - leaves + p)

    def prepare(height, p, row):
        mid_g[row], mid_f[row] = merge(mi[row], mb[row], mk[row], mc[row])

    def upward(height, p, row):
        gs[first(height) + p] = dot3(mid_g[row], pair_of(height, p))

    def aside(height, p, row):
        acc[row] = dot3(mid_f[row], pair_of(height, p))

    lag = jnp.where(inner, INNER_LAG, END_LAG)

    def step(t, carry):
        @pl.when((t < leaves) & inner)
        def _():
            inv_end_recv = remote(inv.at[t], slot(t, end_z), inv_s.at[t], inv_end_r.at[t], {"rhs": end_z})
            inv_end_recv.wait_recv()
            forward(t).start()
            inv_to_pair(t).wait_send()

            @pl.when(t + OWN_AHEAD < leaves)
            def _():
                inv_to_pair(t + OWN_AHEAD).start()

        @pl.when((t < leaves) & end)
        def _():
            inv_to_mid(t).wait_send()
            rhs_to_mid(t).wait_send()

            @pl.when(t + END_AHEAD < leaves)
            def _():
                inv_to_mid(t + END_AHEAD).start()
                rhs_to_mid(t + END_AHEAD).start()

        l = t - lag

        @pl.when((l >= 0) & (l < leaves))
        def _():
            visits(l, prepare)

            @pl.when(inner)
            def _():
                remote(inv.at[l], slot(l, pair_z), inv_s.at[l], inv_mid_r.at[l], {"rhs": pair_z}).wait_recv()
                remote(slot(l, end_z), slot(l, pair_end), fwd_s.at[l], fwd_r.at[l], {"rhs": pair_z}).wait_recv()
                remote(rhs.at[l], rhs_far.at[l], rhs_s.at[l], rhs_r.at[l], {"rhs": end_z}).wait_recv()
                both = jnp.concatenate([rhs_v[l], rhs_far[l]], axis=1)
                solved = jnp.dot(inv_v[l], both, preferred_element_type=f32).astype(bf16)
                vals_far[l] = solved[:, cols:]
                result(l).start()
                vals[l] = solved[:, :cols]

            @pl.when(end)
            def _():
                remote(vals_far.at[l], vals.at[l], res_s.at[l], res_r.at[l], {"rhs": mid_z}).wait_recv()

            vals_copy(l).start()
            mine = lax.dot_general(basis_v[l], vals[l], TRANSPOSED, preferred_element_type=f32)
            proj[l] = mine
            gs[l] = dot3(coarse_v[l], mine)
            visits(l, upward)

            @pl.when(l < leaves - 1)
            def _():
                visits(l, aside)

        return carry

    lax.fori_loop(0, leaves + END_LAG, step, 0)

    def exchange(height):
        partner = pos + jnp.where(lax.rem(pos // (1 << (height - 1)), 2) == 0, 1, -1) * (1 << (height - 1))
        return remote(top_g.at[height - 1], top_in.at[height - 1], ex_s.at[height - 1], ex_r.at[height - 1],
                      {"leaf": partner})

    top_g[0] = gs[first(levels)]
    side = [lax.rem(pos // (1 << (height - 1)), 2) for height in range(1, depth + 1)]

    def stacked(height):
        i = height - 1
        left = side[i] == 0
        return jnp.concatenate([jnp.where(left, top_g[i], top_in[i]), jnp.where(left, top_in[i], top_g[i])], axis=0)

    def half(height):
        return pl.ds(pl.multiple_of(side[height - 1] * rank, rank), rank)

    def top_aside(height):
        i = height - 1
        lower = pl.ds(pl.multiple_of((side[i] + 1) * rank, rank), rank)
        top_a[i] = dot3(top_m[i, lower, :], stacked(height))

    for height in range(1, depth + 1):
        i = height - 1
        exchange(height).start()
        if height == 1:
            visits(leaves - 1 + jnp.int32(0), aside)
        else:
            top_aside(height - 1)

        @pl.when(lax.rem(pos, 1 << height) != 1 << i)
        def _():
            for copy in top_copies(height, 1):
                copy.wait_recv()

        exchange(height).wait_recv()
        if height < depth:
            top_g[height] = dot3(top_m[i, 0:rank, :], stacked(height))
    top_aside(depth)
    down = top_a[depth - 1]
    for height in range(depth - 1, 0, -1):
        i = height - 1
        down = top_a[i] + dot3(top_w[i, half(height), :], down)
    zs[first(levels)] = down

    for height in range(levels, 0, -1):
        def lower(p, carry):
            row = first(height) - leaves + p
            halves = acc[row] + dot3(mk[row], zs[first(height) + p])
            for j in range(2):
                part = halves[j * rank:(j + 1) * rank]
                if height > 1:
                    zs[first(height - 1) + 2 * p + j] = part
                else:
                    diff_out[2 * p + j] = (proj[2 * p + j] - part).astype(bf16)
            return carry

        lax.fori_loop(0, leaves >> height, lower, 0)

    for height in range(1, depth + 1):
        exchange(height).wait_send()

        @pl.when(lax.rem(pos, 1 << height) == 1 << (height - 1))
        def _():
            def done(k, carry):
                for copy in top_copies(height, k):
                    copy.wait_send()
                return carry

            lax.fori_loop(1, 1 << height, done, 0)

    def finish(l, carry):
        vals_copy(l).wait()

        @pl.when(inner)
        def _():
            forward(l).wait_send()
            result(l).wait_send()

        return carry

    lax.fori_loop(0, leaves, finish, 0)


def output_kernel(vals, back, diff, out):
    out[0] = vals[0].astype(f32) - jnp.dot(back[0], diff[0], preferred_element_type=f32)


def per_device(leaf_total, rhs_cols, leaf_inv, leaf_basis, leaf_back, leaf_coarse, mid_inv, mid_basis,
               mid_back, mid_coarse, top_inv, top_basis, top_back, top_coarse):
    leaves, rows, width = leaf_inv.shape
    rank, cols = leaf_basis.shape[2], rhs_cols.shape[1]
    depth = leaf_total.bit_length() - 1
    blocks = rhs_cols.reshape(leaves, width, cols)
    dma = pltpu.SemaphoreType.DMA
    mids = mid_inv.shape[0]
    operands = (blocks, leaf_inv, leaf_basis, leaf_coarse, mid_inv, mid_basis, mid_back, mid_coarse,
                top_inv, top_basis, top_back, top_coarse)
    small = [pltpu.VMEM(a.shape, a.dtype) for a in operands[2:]]
    vals, diff = pl.pallas_call(
        functools.partial(tree_kernel, leaf_total),
        out_shape=(jax.ShapeDtypeStruct((leaves, width, cols), bf16),
                   jax.ShapeDtypeStruct((leaves, rank, cols), bf16)),
        in_specs=[pl.BlockSpec(memory_space=pl.ANY)] * len(operands),
        out_specs=(pl.BlockSpec(memory_space=pl.ANY), pl.BlockSpec(memory_space=pltpu.VMEM)),
        scratch_shapes=[
            pltpu.VMEM((leaves, width, width), bf16),
            pltpu.VMEM((leaves, width, cols), bf16),
            pltpu.VMEM((leaves, width, cols), bf16),
            pltpu.VMEM((leaves, width, cols), bf16),
            pltpu.VMEM((leaves, width, cols), bf16),
            *small,
            pltpu.VMEM((mids, rank, 2 * rank), f32),
            pltpu.VMEM((mids, 2 * rank, 2 * rank), f32),
            pltpu.VMEM((2 * leaves, rank, cols), f32),
            pltpu.VMEM((mids, 2 * rank, cols), f32),
            pltpu.VMEM((leaves, rank, cols), f32),
            pltpu.VMEM((2 * leaves, rank, cols), f32),
            pltpu.VMEM((depth, 3 * rank, 2 * rank), f32),
            pltpu.VMEM((depth, 2 * rank, rank), f32),
            pltpu.VMEM((depth, rank, cols), f32),
            pltpu.VMEM((depth, rank, cols), f32),
            pltpu.VMEM((depth, rank, cols), f32),
            dma((len(operands),)),
            *[dma((leaves,)) for _ in range(10)],
            dma((2, leaf_total)),
            dma((2, depth)),
            dma((depth,)),
            dma((depth,)),
        ],
        compiler_params=pltpu.CompilerParams(
            collective_id=0, has_side_effects=True, vmem_limit_bytes=56 * 1024 * 1024),
    )(*operands)

    def block(*shape):
        return pl.BlockSpec((1,) + shape, lambda i: (i, 0, 0))

    result = pl.pallas_call(
        output_kernel,
        grid=(leaves,),
        out_shape=jax.ShapeDtypeStruct((leaves, width, cols), f32),
        in_specs=[block(width, cols), block(width, rank), block(rank, cols)],
        out_specs=block(width, cols),
    )(vals, leaf_back, diff)
    return result.reshape(leaves * width, cols)


def solution(mesh):
    shards = P("leaf", None, None)
    return jax.shard_map(
        functools.partial(per_device, mesh.shape["leaf"]),
        mesh=mesh,
        in_specs=(P("leaf", "rhs"), P("leaf", "rhs", None)) + (shards,) * 11,
        out_specs=P("leaf", "rhs"),
        check_vma=False,
    )
```
